512 devices in a mesh: sub: 128 (over y, z, core), grp: 4 (over x).
Axes of the slice: x: 4, y: 8, z: 8, core: 2. Of those that a mesh axis runs over, the one named last changes fastest.
Arguments:
- gradients: bfloat16 [9, 12, 4, 65536], P(None, None, 'grp', 'sub'), may hold values from -1.75 to 1.75
- moduli: bfloat16 [9, 4, 65536], P(None, 'grp', 'sub'), may hold values from 0.5 to 4
- diag_terms: bfloat16 [12, 4, 65536], P(None, 'grp', 'sub'), may hold values from 0.29882812 to 3
- counts: int32 [4, 128, 128], P('grp', 'sub'), may hold values from 1 to 12, as said below
- targets: int32 [4, 65536], P('grp', 'sub'), may hold values from 0 to 127
- compliance: float32 [144, 4, 16384], P(None, 'grp', 'sub'), as said below
- neighbours: int32 [4, 128, 128], P('grp', 'sub'), may hold values from 0 to 127, each once within a row
- rhs: float32 [12, 4, 16384], P(None, 'grp', 'sub'), may hold values from -6 to 6
Outputs:
- multipliers: float32 [12, 4, 16384], P(None, 'grp', 'sub')
- stiffness: float32 [144, 4, 16384], P(None, 'grp', 'sub')
The draws below stay inside these ranges and needn't reach their ends.
Inputs may be any that keep to these rules, and one draw needn't show every extreme that they name: Each row counts[g, i, :] sums to 512, every entry is at least 1 and no entry exceeds 12; in every group one owner receives exactly 12 elements from every device of the group. `compliance`: every 12 x 12 block is symmetric positive definite.
All inputs are finite; a program needn't handle non-finite values.
Results may differ from the reference program's by a relative error of at most 0.0003.
Values may be sent and summed in bfloat16 or wider, within the bound.
A program may use at most 64 MiB of HBM per device.

```python
import math
import jax
import jax.numpy as jnp
from jax import lax

E_DEV = 512
ITERS = 2
CAP = 12
COLS = 128
ELEMS = 65536
LAMS = 16384
N_SUB = 128
N_GRP = 4


def draw_counts(key, part):
    key = jax.random.fold_in(key, 5)
    hot_key, pair_key = jax.random.split(key)
    hottest = jax.random.randint(hot_key, (N_GRP, 1, 1), 0, N_SUB)
    others = N_SUB - 1
    remaining = E_DEV - CAP
    base = remaining // others
    extra = remaining % others
    spread = min(base - 1, CAP - base - 1)
    swings = jax.random.randint(pair_key, (N_GRP, N_SUB, others // 2 + 1), 0, spread + 1)
    order = jnp.arange(others)
    paired = (order < 2 * (others // 2)).astype(jnp.int32)
    signs = jnp.where(order % 2 == 0, 1, -1) * paired
    amounts = base + (order < extra).astype(jnp.int32) + signs[None, None, :] * swings[:, :, order // 2]
    peers = jnp.arange(N_SUB)[None, None, :]
    slots = jnp.clip(jnp.where(peers < hottest, peers, peers - 1), 0, others - 1)
    slots = jnp.broadcast_to(slots, (N_GRP, N_SUB, N_SUB))
    picked = jnp.take_along_axis(amounts, slots, axis=2)
    return jnp.where(peers == hottest, CAP, picked).astype(jnp.int32)


def draw_compliance(key, part):
    key = jax.random.fold_in(key, 9)
    off_key, diag_key = jax.random.split(key)
    shape = (12, 12, N_GRP, N_SUB * COLS)
    off = jax.random.uniform(off_key, shape, jnp.float32, -0.08, 0.08)
    diagonal = jax.random.uniform(diag_key, (12, N_GRP, N_SUB * COLS), jnp.float32, 2.0, 4.0)
    symmetric = off + jnp.transpose(off, (1, 0, 2, 3))
    identity = jnp.eye(12, dtype=jnp.float32)[:, :, None, None]
    blocks = symmetric * (1.0 - identity) + identity * diagonal[None]
    return blocks.reshape(144, N_GRP, N_SUB * COLS)


def place_ends(drawn, own_key, least, high):
    extent = drawn.shape
    place = [jax.random.randint(jax.random.fold_in(own_key, axis), (), 0, extent[axis]) for axis in range(len(extent))]
    drawn = drawn.at[tuple(place)].set(least)
    longest = extent.index(max(extent))
    place[longest] = (place[longest] + 1) % extent[longest]
    return drawn.at[tuple(place)].set(high)


def level_of(own_key, shape, pieces, low, top_value):
    gain = 1.0
    for axis_at, shards_of in pieces:
        heights = jax.random.uniform(jax.random.fold_in(jax.random.fold_in(own_key, 6), axis_at), (shards_of,), jnp.float32, low / len(pieces), top_value / len(pieces))
        gain = gain * jnp.repeat(jnp.exp(heights), shape[axis_at] // shards_of).reshape((-1,) + (1,) * (len(shape) - 1 - axis_at))
    return gain


def noise(key, extent, deviation, most, shards=(), held_as=jnp.bfloat16):
    loudness = level_of(key, extent, shards, -0.22, 0.18) if shards else 1.0
    drawn = jax.random.normal(key, extent, jnp.float32) * deviation * loudness
    return jnp.minimum(jnp.maximum(drawn, -most), most).astype(held_as)


def setup_inputs(seed: int = 0) -> dict:
    key_list = jax.random.split(jax.random.key(seed), 9)
    return {
        "gradients": noise(key_list[0], (9, 12, N_GRP, ELEMS), 12 ** -0.5, 1.75, ((2, 4), (3, 128))),
        "moduli": jnp.clip(jnp.exp(math.log(4.0) - 2.0794415 * jax.random.uniform(key_list[1], (9, N_GRP, ELEMS), jnp.float32) ** level_of(key_list[1], (9, N_GRP, ELEMS), ((1, 4), (2, 128)), -0.2, 0.2)), 0.5, 4.0).astype(jnp.bfloat16),
        "diag_terms": jnp.clip(jnp.exp(math.log(3.0) - 2.306499 * jax.random.uniform(key_list[2], (12, N_GRP, ELEMS), jnp.float32) ** level_of(key_list[2], (12, N_GRP, ELEMS), ((1, 4), (2, 128)), -0.2, 0.2)), 0.29882812, 3.0).astype(jnp.bfloat16),
        "counts": draw_counts(jax.random.fold_in(key_list[8], 71), 0),
        "targets": place_ends(jax.random.randint(key_list[4], (N_GRP, ELEMS), 0, COLS), jax.random.fold_in(key_list[4], 1), 0, COLS - 1).astype(jnp.int32),
        "compliance": draw_compliance(jax.random.fold_in(key_list[8], 71), 0),
        "neighbours": jax.vmap(lambda own: jax.random.permutation(own, COLS))(jax.random.split(key_list[6], N_GRP * N_SUB)).reshape((N_GRP, N_SUB, COLS)).astype(jnp.int32),
        "rhs": noise(key_list[7], (12, N_GRP, LAMS), 1.0, 6.0, ((1, 4), (2, 128)), jnp.float32),
    }


def tangent(grads, moduli_part, extra):
    grads_f = grads.astype(jnp.float32)
    mods_f = moduli_part.astype(jnp.float32)
    blocks = jnp.zeros((12, 12, grads.shape[2]), jnp.float32)
    for entry in range(9):
        weighted = grads_f[entry] * mods_f[entry][None, :]
        blocks = blocks + grads_f[entry][:, None, :] * weighted[None, :, :]
    identity = jnp.eye(12, dtype=jnp.float32)
    blocks = blocks + identity[:, :, None] * extra.astype(jnp.float32)[:, None, :]
    return blocks.reshape(144, -1)


def column_apply(mats, vectors):
    shaped = mats.reshape((12, 12) + vectors.shape[1:])
    return jnp.sum(shaped * vectors[None], axis=1)


def coupled_all(mats, vectors, neighbours, inverse):
    here = column_apply(mats, vectors)
    moved = jnp.take_along_axis(vectors, inverse[None], axis=3)
    rolled = jnp.roll(mats, -1, axis=1)
    there = column_apply(rolled, moved)
    return here + jnp.take_along_axis(there, neighbours[None], axis=3)


def reference(gradients, moduli, diag_terms, counts, targets, compliance, neighbours, rhs):
    groups = []
    for group in range(N_GRP):
        def sender(total, index):
            start = index * E_DEV
            grads = lax.dynamic_slice_in_dim(gradients[:, :, group], start, E_DEV, 2)
            mods = lax.dynamic_slice_in_dim(moduli[:, group], start, E_DEV, 1)
            extra = lax.dynamic_slice_in_dim(diag_terms[:, group], start, E_DEV, 1)
            patches = lax.dynamic_slice_in_dim(targets[group], start, E_DEV, 0).astype(jnp.int32)
            sent = lax.dynamic_index_in_dim(counts[group], index, 0, keepdims=False)
            ends = jnp.cumsum(sent).astype(jnp.int32)
            position = jnp.arange(E_DEV, dtype=jnp.int32)
            owner = jnp.sum((ends[None, :] <= position[:, None]).astype(jnp.int32), axis=1).astype(jnp.int32)
            blocks = tangent(grads, mods, extra)
            return total.at[:, owner * COLS + patches].add(blocks), None

        empty = jnp.zeros((144, N_SUB * COLS), jnp.float32)
        summed, _ = lax.scan(sender, empty, jnp.arange(N_SUB, dtype=jnp.int32))
        groups.append(summed)
    stiffness = jnp.stack(groups, axis=1)

    shape4 = (N_GRP, N_SUB, COLS)
    lumped = stiffness.reshape((144,) + shape4) + jnp.eye(12, dtype=jnp.float32).reshape(144, 1, 1, 1)
    comp = compliance.reshape((144,) + shape4)
    group_idx = jnp.arange(N_GRP, dtype=jnp.int32)[:, None, None]
    sub_idx = jnp.arange(N_SUB, dtype=jnp.int32)[None, :, None]
    column_idx = jnp.broadcast_to(jnp.arange(COLS, dtype=jnp.int32)[None, None, :], shape4)
    inverse = jnp.zeros(shape4, jnp.int32).at[group_idx, sub_idx, neighbours].set(column_idx)

    resid = rhs.reshape((12,) + shape4)
    multipliers = jnp.zeros_like(resid)
    precond = coupled_all(lumped, resid, neighbours, inverse)
    direction = precond
    rz_now = jnp.sum(resid * precond)
    for iteration in range(ITERS):
        image = coupled_all(comp, direction, neighbours, inverse)
        alpha = rz_now / jnp.sum(direction * image)
        multipliers = multipliers + alpha * direction
        resid = resid - alpha * image
        if iteration + 1 < ITERS:
            precond = coupled_all(lumped, resid, neighbours, inverse)
            rz_next = jnp.sum(resid * precond)
            direction = precond + (rz_next / rz_now) * direction
            rz_now = rz_next
    return multipliers.reshape(12, N_GRP, N_SUB * COLS), stiffness
```

```python
import jax
import jax.numpy as jnp
from jax import lax
from jax.experimental import pallas as pl
from jax.experimental.pallas import tpu as pltpu
from jax.sharding import PartitionSpec as P

MESH = pl.DeviceIdType.MESH
F32, BF16, I32 = jnp.float32, jnp.bfloat16, jnp.int32
N = 12
HALF = 7
ROW, COL, GRP = 16, 8, 4
SUB = ROW * COL
ELEMS = 512
COLS = 128
CAP = 12
WORDS = 42
LANES_OF = 3
ROWS_OF = CAP // LANES_OF
SLOT_ROWS = SUB * ROWS_OF


def dot_nt(a, b):
    return lax.dot_general(a, b, (((1,), (1,)), ((), ())), preferred_element_type=F32)


def tangents(grads, mods, diag):
    sums = [None] * HALF
    for m in range(9):
        g = grads[m]
        weighted = g * mods[m : m + 1]
        wrapped = jnp.concatenate([g, g[:6]], axis=0)
        for d in range(HALF):
            rows = 6 if d == 6 else N
            term = weighted[:rows] * wrapped[d : d + rows]
            sums[d] = term if sums[d] is None else sums[d] + term
    sums[0] = sums[0] + diag
    return sums


def apply_half(k, v):
    twice = jnp.concatenate([v, v], axis=0)
    out = k[0] * v
    for d in range(1, 6):
        out = out + k[d] * twice[d : d + N]
        back = k[d] * v
        back = jnp.concatenate([back, back], axis=0)
        out = out + back[N - d : 2 * N - d]
    k6 = jnp.concatenate([k[6], k[6]], axis=0)
    return out + k6 * twice[6 : 6 + N]


def apply_full(k_ref, v):
    out = None
    for b in range(N):
        term = k_ref[b * N : (b + 1) * N, :] * v[b : b + 1]
        out = term if out is None else out + term
    return out


def combine(slots, count):
    row = lax.broadcasted_iota(I32, (8, COLS), 0)
    top = slots[0, 4:5]
    for i in range(1, count):
        top = jnp.maximum(top, slots[i, 4:5])
    total = None
    for i in range(count):
        term = weigh(slots[i], slots[i, 4:5] / top, row)
        total = term if total is None else total + term
    return jnp.where(row == 4, jnp.broadcast_to(top, (8, COLS)), total)


def weigh(block, ratio, row):
    ratio = jnp.broadcast_to(ratio, (8, COLS))
    square = ratio * ratio
    factor = jnp.where(row == 1, ratio, jnp.where(row == 2, square, square * ratio))
    return block * jnp.where(row == 0, 1.0, factor)


def kernel(
    grads, mods, diag, counts, targets, comp, neigh, rhs,
    lam_out, stiff_out,
    g_v, m_v, d_v, c_v, t_v, n_v, r_v, own_c, near_c,
    sel, rhs_h, rhs_l, send, recv, half_own, half_near, stiff_v, lam_v,
    mine, slots_a, slots_b, slots_c,
    in_sem, row_sem, comp_sems, out_sems, local_sem, move_sems, half_sems, sem_a, sem_b, sem_c,
):
    me, grp = lax.axis_index("sub"), lax.axis_index("grp")
    y, zc = me // ROW, me % ROW
    behind = (me, (grp + GRP - 1) % GRP)

    barrier = pltpu.get_barrier_semaphore()

    def greet(device):
        pl.semaphore_signal(barrier, inc=1, device_id=device, device_id_type=MESH)

    for d in range(1, COL):
        greet((((y + d) % COL) * ROW + zc, grp))
    for d in range(1, ROW):
        greet((y * ROW + (zc + d) % ROW, grp))
    for d in range(1, GRP):
        greet((me, (grp + d) % GRP))

    loads = [(grads, g_v), (mods, m_v), (diag, d_v), (counts, c_v), (targets, t_v),
             (neigh, n_v), (rhs, r_v), (comp, own_c)]
    loads = [pltpu.make_async_copy(a, b, in_sem.at[i]) for i, (a, b) in enumerate(loads)]
    for copy in loads:
        copy.start()
    for copy in loads[:5]:
        copy.wait()

    mods_f = m_v[...].astype(F32)
    for t in range(ELEMS // COLS):
        at = pl.ds(t * COLS, COLS)
        tile = tangents(
            [g_v[m, :, at].astype(F32) for m in range(9)],
            mods_f[:, t * COLS : (t + 1) * COLS],
            d_v[:, at].astype(F32),
        )
        biggest = jnp.max(tile[0], axis=0, keepdims=True)
        step = (biggest * 1.01).astype(BF16).astype(F32)
        scale = 32768.0 / step
        meta = jnp.concatenate(
            [t_v[:, at].astype(F32), step * 512.0, jnp.zeros((4, COLS), F32)], axis=0
        )
        high = [jnp.floor(tile[d] * scale + 0.5) for d in (0, 2, 4, 6)]
        low = [jnp.floor(tile[d] * scale + 0.5) for d in (1, 3, 5)] + [meta]
        for half, values in enumerate((high, low)):
            values = jnp.concatenate(values, axis=0)
            upper = jnp.floor(values * (1.0 / 256.0)) * 256.0
            for piece, ref in ((upper, rhs_h), (values - upper, rhs_l)):
                for j in range(LANES_OF):
                    parts = [piece]
                    if j:
                        parts = [jnp.zeros((j * WORDS, COLS), F32)] + parts
                    parts = parts + [jnp.zeros((COLS - (j + 1) * WORDS, COLS), F32)]
                    ref[half * COLS : (half + 1) * COLS, pl.ds(j * ELEMS + t * COLS, COLS)] = (
                        jnp.concatenate(parts, axis=0).astype(BF16)
                    )

    line = lax.broadcasted_iota(I32, (SLOT_ROWS, COLS), 0)
    lane = lax.broadcasted_iota(I32, (SLOT_ROWS, COLS), 1)
    per_peer = jnp.broadcast_to(c_v[...].astype(F32), (COLS, SUB)).astype(BF16)
    first = dot_nt((lane < line // ROWS_OF).astype(F32).astype(BF16), per_peer)
    listed = dot_nt((lane == line // ROWS_OF).astype(F32).astype(BF16), per_peer)
    place = ((line % ROWS_OF) * LANES_OF).astype(F32)
    lane_f = lane.astype(F32)
    for j in range(LANES_OF):
        wanted = jnp.where(place + j < listed, first + place + j, -1.0)
        for t in range(ELEMS // COLS):
            hit = jnp.where(wanted == lane_f + t * COLS, 1.0, 0.0)
            sel[:, pl.ds(j * ELEMS + t * COLS, COLS)] = hit.astype(BF16)

    pl.semaphore_wait(barrier, ROW + COL + GRP - 3)
    for d in range(1, COL):
        pl.semaphore_signal(
            row_sem, inc=1, device_id=(((y + d) % COL) * ROW + zc, grp), device_id_type=MESH
        )
    for copy in loads[5:]:
        copy.wait()
    comp_copy = pltpu.make_async_remote_copy(
        own_c, near_c, comp_sems.at[0], comp_sems.at[1], device_id=behind, device_id_type=MESH
    )
    comp_copy.start()

    for c in range(4):
        rows = pl.ds(c * 128, 128)
        packed = dot_nt(sel[rows, :], rhs_h[...]) + dot_nt(sel[rows, :], rhs_l[...])
        packed = packed.astype(I32)
        words = (packed[:, :COLS] << 16) | (packed[:, COLS:] & 0xFFFF)
        send[pl.ds(c * 32, 32)] = words.reshape(32, ROWS_OF, COLS)

    pl.semaphore_wait(row_sem, COL - 1)
    local = pltpu.make_async_copy(send.at[me], recv.at[me], local_sem)
    local.start()

    @pl.loop(1, SUB)
    def _(d):
        peer = me ^ d
        pltpu.make_async_remote_copy(
            send.at[peer], recv.at[me], move_sems.at[0], move_sems.at[1],
            device_id=(peer, grp), device_id_type=MESH,
        ).start()

    comp_copy.wait()
    facing = jnp.broadcast_to(n_v[...], (8, COLS))

    def moved(block):
        rows = block.shape[0]
        if rows % 8:
            block = jnp.concatenate([block, jnp.zeros((8 - rows % 8, COLS), F32)], axis=0)
        parts = [
            jnp.take_along_axis(block[i : i + 8], facing, axis=1)
            for i in range(0, block.shape[0], 8)
        ]
        return jnp.concatenate(parts, axis=0)[:rows]

    both_c = own_c[...] + moved(near_c[...])
    unit = both_c[0:1]
    for a in range(1, N):
        unit = jnp.maximum(unit, both_c[a * (N + 1) : a * (N + 1) + 1])
    own_c[...] = both_c / unit

    local.wait()
    others = recv.at[pl.ds(0, SUB - 1)]
    pltpu.make_async_copy(others, others, move_sems.at[1]).wait()

    words = recv[...].reshape(SLOT_ROWS, COLS)
    high = words >> 16
    low = (words << 16) >> 16
    pieces = [high >> 8, high & 255, low >> 8, low & 255]
    pieces = jnp.concatenate([p.astype(F32).astype(BF16) for p in pieces], axis=1)
    meta = low.astype(F32).T
    patch = lax.broadcasted_iota(I32, (COLS, SLOT_ROWS), 0).astype(F32)
    lane = lax.broadcasted_iota(I32, (COLS, COLS), 1)
    sums = [jnp.zeros((COLS, COLS), F32)] * 2
    for j in range(LANES_OF):
        target = meta[j * WORDS + 36 : j * WORDS + 37]
        code = meta[j * WORDS + 37 : j * WORDS + 38]
        step = jnp.where(code < 0.0, code + 65536.0, code) * (1.0 / 512.0)
        hit = jnp.where(patch == target, step, 0.0).astype(BF16)
        part = jnp.dot(hit, pieces, preferred_element_type=F32)
        here = (lane >= j * WORDS) & (lane < (j + 1) * WORDS)
        for half in range(2):
            upper = part[:, half * 256 : half * 256 + 128]
            lower = part[:, half * 256 + 128 : half * 256 + 256]
            sums[half] = sums[half] + jnp.where(here, upper * 256.0 + lower, 0.0)
    for half in range(2):
        turned = sums[half].T * (1.0 / 32768.0)
        folded = turned[:WORDS] + turned[WORDS : 2 * WORDS] + turned[2 * WORDS : 3 * WORDS]
        half_own[half * 48 : half * 48 + 48, :] = jnp.concatenate(
            [folded, jnp.zeros((6, COLS), F32)], axis=0
        )
    half_copy = pltpu.make_async_remote_copy(
        half_own, half_near, half_sems.at[0], half_sems.at[1], device_id=behind, device_id_type=MESH
    )
    half_copy.start()
    start_of = [0, 48, 12, 60, 24, 72, 36]
    for a in range(N):
        for b in range(N):
            d = (b - a) % N
            source = start_of[d] + a % (6 if d == 6 else N) if d < HALF else start_of[N - d] + b
            stiff_v[a * N + b : a * N + b + 1, :] = half_own[source : source + 1, :]
    stiff_copy = pltpu.make_async_copy(stiff_v, stiff_out, out_sems.at[0])
    stiff_copy.start()
    half_copy.wait()

    both = half_own[...] + moved(half_near[...])
    k = [both[s : s + (6 if d == 6 else N)] for d, s in enumerate(start_of)]
    k[0] = k[0] + 2.0

    resid = r_v[...]
    precond = apply_half(k, resid)
    image = apply_full(own_c, precond)
    again = apply_half(k, image)
    image_again = apply_full(own_c, again)

    def inner(a, b):
        return jnp.sum(a * b, axis=0, keepdims=True)

    mine[...] = jnp.concatenate(
        [inner(resid, precond), inner(precond, image), inner(image, again),
         inner(again, image_again), unit, jnp.zeros((3, COLS), F32)], axis=0,
    )

    def spread(slots, count, here, device_of, sems):
        slots[here] = mine[...]
        for d in range(1, count):
            pltpu.make_async_remote_copy(
                mine, slots.at[here], sems.at[0], sems.at[1],
                device_id=device_of((here + d) % count), device_id_type=MESH,
            ).start()
        rest = slots.at[pl.ds(0, count - 1)]
        pltpu.make_async_copy(rest, rest, sems.at[1]).wait()
        pltpu.make_async_copy(rest, rest, sems.at[0]).wait()
        mine[...] = combine(slots, count)

    spread(slots_a, ROW, zc, lambda i: (y * ROW + i, grp), sem_a)
    spread(slots_b, COL, y, lambda i: (i * ROW + zc, grp), sem_b)
    spread(slots_c, GRP, grp, lambda i: (me, i), sem_c)

    total = mine[...]
    row = lax.broadcasted_iota(I32, (8, COLS), 0)
    top = jnp.max(total[4:5], axis=1, keepdims=True)
    total = jnp.sum(weigh(total, total[4:5] / top, row), axis=1, keepdims=True)
    rz, pq, quq, uw = (total[i : i + 1] for i in range(4))
    alpha = rz / pq
    rz_next = alpha * alpha * quq - rz
    grown = 1.0 + rz_next / rz
    alpha_next = rz_next / (alpha * alpha * uw - grown * grown * pq)
    lam_v[...] = (
        (alpha + alpha_next * grown) / top * precond
        - alpha_next * alpha / top * (unit / top) * again
    )
    lam_copy = pltpu.make_async_copy(lam_v, lam_out, out_sems.at[1])
    lam_copy.start()
    pltpu.make_async_copy(others, others, move_sems.at[0]).wait()
    stiff_copy.wait()
    lam_copy.wait()


def per_device(gradients, moduli, diag_terms, counts, targets, compliance, neighbours, rhs):
    vmem = lambda shape, dtype=F32: pltpu.VMEM(shape, dtype)
    dma = pltpu.SemaphoreType.DMA
    lam, stiff = pl.pallas_call(
        kernel,
        out_shape=(
            jax.ShapeDtypeStruct((N, COLS), F32),
            jax.ShapeDtypeStruct((N * N, COLS), F32),
        ),
        in_specs=[pl.BlockSpec(memory_space=pl.ANY)] * 8,
        out_specs=[pl.BlockSpec(memory_space=pl.ANY)] * 2,
        scratch_shapes=[
            vmem((9, N, ELEMS), BF16),
            vmem((9, ELEMS), BF16),
            vmem((N, ELEMS), BF16),
            vmem((1, SUB), I32),
            vmem((1, ELEMS), I32),
            vmem((1, COLS), I32),
            vmem((N, COLS)),
            vmem((N * N, COLS)),
            vmem((N * N, COLS)),
            vmem((SLOT_ROWS, LANES_OF * ELEMS), BF16),
            vmem((2 * COLS, LANES_OF * ELEMS), BF16),
            vmem((2 * COLS, LANES_OF * ELEMS), BF16),
            vmem((SUB, ROWS_OF, COLS), I32),
            vmem((SUB, ROWS_OF, COLS), I32),
            vmem((96, COLS)),
            vmem((96, COLS)),
            vmem((N * N, COLS)),
            vmem((N, COLS)),
            vmem((8, COLS)),
            vmem((ROW, 8, COLS)),
            vmem((COL, 8, COLS)),
            vmem((GRP, 8, COLS)),
            dma((8,)),
            pltpu.SemaphoreType.REGULAR,
            dma((2,)),
            dma((2,)),
            dma,
            dma((2,)),
            dma((2,)),
            dma((2,)),
            dma((2,)),
            dma((2,)),
        ],
        compiler_params=pltpu.CompilerParams(
            collective_id=0, has_side_effects=True, vmem_limit_bytes=32 * 1024 * 1024
        ),
    )(
        gradients[:, :, 0, :],
        moduli[:, 0, :],
        diag_terms[:, 0, :],
        counts[0],
        targets,
        compliance[:, 0, :],
        neighbours[0],
        rhs[:, 0, :],
    )
    return lam[:, None, :], stiff[:, None, :]


def solution(mesh):
    in_specs = (
        P(None, None, "grp", "sub"),
        P(None, "grp", "sub"),
        P(None, "grp", "sub"),
        P("grp", "sub", None),
        P("grp", "sub"),
        P(None, "grp", "sub"),
        P("grp", "sub", None),
        P(None, "grp", "sub"),
    )
    out_specs = (P(None, "grp", "sub"), P(None, "grp", "sub"))
    return jax.shard_map(
        per_device, mesh=mesh, in_specs=in_specs, out_specs=out_specs, check_vma=False
    )
```

```python
import jax
import jax.numpy as jnp
from jax import lax
from jax.experimental import pallas as pl
from jax.experimental.pallas import tpu as pltpu
from jax.sharding import PartitionSpec as P

MESH = pl.DeviceIdType.MESH
F32, BF16, I32 = jnp.float32, jnp.bfloat16, jnp.int32
N = 12
HALF = 7
ROW, COL, GRP = 16, 8, 4
SUB = ROW * COL
ELEMS = 512
COLS = 128
CAP = 12
WORDS = 42
LANES_OF = 3
ROWS_OF = CAP // LANES_OF
SLOT_ROWS = SUB * ROWS_OF


def hops(step, size):
    return min(step % size, -step % size)


ROW_STEPS = sorted(((z, c) for z in range(8) for c in range(2) if z or c), key=lambda s: -hops(s[0], 8))
FAN_STEPS = sorted(
    ((y, x) for y in range(COL) for x in range(GRP) if y or x),
    key=lambda s: -hops(s[0], COL) - hops(s[1], GRP),
)
ROWS_ORDER = list(range(1, COL))
COL_STEPS = sorted(range(1, COL), key=lambda s: -hops(s, COL))


def dot_nt(a, b):
    return lax.dot_general(a, b, (((1,), (1,)), ((), ())), preferred_element_type=F32)


def tangents(grads, mods, diag):
    sums = [None] * HALF
    for m in range(9):
        g = grads[m]
        weighted = g * mods[m : m + 1]
        wrapped = jnp.concatenate([g, g[:6]], axis=0)
        for d in range(HALF):
            rows = 6 if d == 6 else N
            term = weighted[:rows] * wrapped[d : d + rows]
            sums[d] = term if sums[d] is None else sums[d] + term
    sums[0] = sums[0] + diag
    return sums


def apply_half(k, v):
    twice = jnp.concatenate([v, v], axis=0)
    out = k[0] * v
    for d in range(1, 6):
        out = out + k[d] * twice[d : d + N]
        back = k[d] * v
        back = jnp.concatenate([back, back], axis=0)
        out = out + back[N - d : 2 * N - d]
    k6 = jnp.concatenate([k[6], k[6]], axis=0)
    return out + k6 * twice[6 : 6 + N]


def apply_full(k_ref, v):
    out = None
    for b in range(N):
        term = k_ref[b * N : (b + 1) * N, :] * v[b : b + 1]
        out = term if out is None else out + term
    return out


def combine(slots, count):
    row = lax.broadcasted_iota(I32, (8, COLS), 0)
    top = slots[0, 4:5]
    for i in range(1, count):
        top = jnp.maximum(top, slots[i, 4:5])
    total = None
    for i in range(count):
        term = weigh(slots[i], slots[i, 4:5] / top, row)
        total = term if total is None else total + term
    return jnp.where(row == 4, jnp.broadcast_to(top, (8, COLS)), total)


def weigh(block, ratio, row):
    ratio = jnp.broadcast_to(ratio, (8, COLS))
    square = ratio * ratio
    factor = jnp.where(row == 1, ratio, jnp.where(row == 2, square, square * ratio))
    return block * jnp.where(row == 0, 1.0, factor)


def kernel(
    grads, mods, diag, counts, targets, comp, neigh, rhs,
    lam_out, stiff_out,
    g_v, m_v, d_v, c_v, t_v, n_v, r_v, own_c, near_c,
    sel, rhs_h, rhs_l, send, recv, half_own, half_near,
    mine, row_sum, slots_a, slots_b,
    in_sem, row_sems, comp_sems, local_sem, move_sems, half_sems, sem_a, sem_b,
):
    me, grp = lax.axis_index("sub"), lax.axis_index("grp")
    y, zc = me // ROW, me % ROW
    behind = (me, (grp + GRP - 1) % GRP)

    z, core = zc // 2, zc % 2

    def at(dy=0, dz=0, dc=0, dx=0):
        row = y if dy == 0 else (y + dy) % COL
        col = z if dz == 0 else (z + dz) % 8
        side = core if dc == 0 else 1 - core
        return row * ROW + col * 2 + side, (grp if dx == 0 else (grp + dx) % GRP)

    barrier = pltpu.get_barrier_semaphore()

    def greet(device):
        pl.semaphore_signal(barrier, inc=1, device_id=device, device_id_type=MESH)

    for dz, dc in ROW_STEPS:
        greet(at(dz=dz, dc=dc))
    for dy in COL_STEPS:
        greet(at(dy=dy))
    for dx in range(1, GRP):
        greet(at(dx=dx))

    loads = [(grads, g_v), (mods, m_v), (diag, d_v), (counts, c_v), (targets, t_v),
             (neigh, n_v), (rhs, r_v), (comp, own_c)]
    loads = [pltpu.make_async_copy(a, b, in_sem.at[i]) for i, (a, b) in enumerate(loads)]
    for copy in loads:
        copy.start()
    for copy in loads[:5]:
        copy.wait()

    mods_f = m_v[...].astype(F32)
    for t in range(ELEMS // COLS):
        here = pl.ds(t * COLS, COLS)
        tile = tangents(
            [g_v[m, :, here].astype(F32) for m in range(9)],
            mods_f[:, t * COLS : (t + 1) * COLS],
            d_v[:, here].astype(F32),
        )
        biggest = jnp.max(tile[0], axis=0, keepdims=True)
        step = (biggest * 1.01).astype(BF16).astype(F32)
        scale = 32768.0 / step
        meta = jnp.concatenate(
            [t_v[:, here].astype(F32), step * 512.0, jnp.zeros((4, COLS), F32)], axis=0
        )
        high = [jnp.floor(tile[d] * scale + 0.5) for d in (0, 2, 4, 6)]
        low = [jnp.floor(tile[d] * scale + 0.5) for d in (1, 3, 5)] + [meta]
        for half, values in enumerate((high, low)):
            values = jnp.concatenate(values, axis=0)
            upper = jnp.floor(values * (1.0 / 256.0)) * 256.0
            for piece, ref in ((upper, rhs_h), (values - upper, rhs_l)):
                for j in range(LANES_OF):
                    parts = [piece]
                    if j:
                        parts = [jnp.zeros((j * WORDS, COLS), F32)] + parts
                    parts = parts + [jnp.zeros((COLS - (j + 1) * WORDS, COLS), F32)]
                    ref[half * COLS : (half + 1) * COLS, pl.ds(j * ELEMS + t * COLS, COLS)] = (
                        jnp.concatenate(parts, axis=0).astype(BF16)
                    )

    line = lax.broadcasted_iota(I32, (SLOT_ROWS, COLS), 0)
    lane = lax.broadcasted_iota(I32, (SLOT_ROWS, COLS), 1)
    per_peer = jnp.broadcast_to(c_v[...].astype(F32), (COLS, SUB)).astype(BF16)
    first = dot_nt((lane < line // ROWS_OF).astype(F32).astype(BF16), per_peer)
    listed = dot_nt((lane == line // ROWS_OF).astype(F32).astype(BF16), per_peer)
    place = ((line % ROWS_OF) * LANES_OF).astype(F32)
    lane_f = lane.astype(F32)
    for j in range(LANES_OF):
        wanted = jnp.where(place + j < listed, first + place + j, -1.0)
        for t in range(ELEMS // COLS):
            hit = jnp.where(wanted == lane_f + t * COLS, 1.0, 0.0)
            sel[:, pl.ds(j * ELEMS + t * COLS, COLS)] = hit.astype(BF16)

    pl.semaphore_wait(barrier, ROW + COL + GRP - 3)
    for dy in COL_STEPS:
        pl.semaphore_signal(
            row_sems.at[COL - dy], inc=1, device_id=at(dy=dy), device_id_type=MESH
        )
    for copy in loads[5:]:
        copy.wait()
    comp_copy = pltpu.make_async_remote_copy(
        own_c, near_c, comp_sems.at[0], comp_sems.at[1], device_id=behind, device_id_type=MESH
    )
    comp_copy.start()

    for c in range(4):
        rows = pl.ds(c * 128, 128)
        packed = dot_nt(sel[rows, :], rhs_h[...]) + dot_nt(sel[rows, :], rhs_l[...])
        packed = packed.astype(I32)
        words = (packed[:, :COLS] << 16) | (packed[:, COLS:] & 0xFFFF)
        send[pl.ds(c * 32, 32)] = words.reshape(32, ROWS_OF, COLS)

    local = pltpu.make_async_copy(send.at[me], recv.at[me], local_sem)
    local.start()

    def post(dy, dz, dc):
        device = at(dy, dz, dc)
        pltpu.make_async_remote_copy(
            send.at[device[0]], recv.at[me], move_sems.at[0], move_sems.at[1],
            device_id=device, device_id_type=MESH,
        ).start()

    for dy in COL_STEPS:
        post(dy, 0, 0)
    for dz, dc in ROW_STEPS:
        post(0, dz, dc)
    for dy in ROWS_ORDER:
        pl.semaphore_wait(row_sems.at[dy], 1)
        for dz, dc in ROW_STEPS:
            post(dy, dz, dc)

    comp_copy.wait()
    facing = jnp.broadcast_to(n_v[...], (8, COLS))

    def moved(block):
        rows = block.shape[0]
        if rows % 8:
            block = jnp.concatenate([block, jnp.zeros((8 - rows % 8, COLS), F32)], axis=0)
        parts = [
            jnp.take_along_axis(block[i : i + 8], facing, axis=1)
            for i in range(0, block.shape[0], 8)
        ]
        return jnp.concatenate(parts, axis=0)[:rows]

    both_c = own_c[...] + moved(near_c[...])
    unit = both_c[0:1]
    for a in range(1, N):
        unit = jnp.maximum(unit, both_c[a * (N + 1) : a * (N + 1) + 1])
    own_c[...] = both_c / unit

    local.wait()
    others = recv.at[pl.ds(0, SUB - 1)]
    pltpu.make_async_copy(others, others, move_sems.at[1]).wait()

    words = recv[...].reshape(SLOT_ROWS, COLS)
    high = words >> 16
    low = (words << 16) >> 16
    pieces = [high >> 8, high & 255, low >> 8, low & 255]
    pieces = jnp.concatenate([p.astype(F32).astype(BF16) for p in pieces], axis=1)
    meta = low.astype(F32).T
    patch = lax.broadcasted_iota(I32, (COLS, SLOT_ROWS), 0).astype(F32)
    lane = lax.broadcasted_iota(I32, (COLS, COLS), 1)
    sums = [jnp.zeros((COLS, COLS), F32)] * 2
    for j in range(LANES_OF):
        target = meta[j * WORDS + 36 : j * WORDS + 37]
        code = meta[j * WORDS + 37 : j * WORDS + 38]
        step = jnp.where(code < 0.0, code + 65536.0, code) * (1.0 / 512.0)
        hit = jnp.where(patch == target, step, 0.0).astype(BF16)
        part = jnp.dot(hit, pieces, preferred_element_type=F32)
        here = (lane >= j * WORDS) & (lane < (j + 1) * WORDS)
        for half in range(2):
            upper = part[:, half * 256 : half * 256 + 128]
            lower = part[:, half * 256 + 128 : half * 256 + 256]
            sums[half] = sums[half] + jnp.where(here, upper * 256.0 + lower, 0.0)
    for half in range(2):
        turned = sums[half].T * (1.0 / 32768.0)
        folded = turned[:WORDS] + turned[WORDS : 2 * WORDS] + turned[2 * WORDS : 3 * WORDS]
        half_own[half * 48 : half * 48 + 48, :] = jnp.concatenate(
            [folded, jnp.zeros((6, COLS), F32)], axis=0
        )
    half_copy = pltpu.make_async_remote_copy(
        half_own, half_near, half_sems.at[0], half_sems.at[1], device_id=behind, device_id_type=MESH
    )
    half_copy.start()
    start_of = [0, 48, 12, 60, 24, 72, 36]
    for a in range(N):
        for b in range(N):
            d = (b - a) % N
            source = start_of[d] + a % (6 if d == 6 else N) if d < HALF else start_of[N - d] + b
            stiff_out[a * N + b] = half_own[source : source + 1, :]
    half_copy.wait()

    both = half_own[...] + moved(half_near[...])
    k = [both[s : s + (6 if d == 6 else N)] for d, s in enumerate(start_of)]
    k[0] = k[0] + 2.0

    resid = r_v[:, 0, :]
    precond = apply_half(k, resid)
    image = apply_full(own_c, precond)
    again = apply_half(k, image)
    image_again = apply_full(own_c, again)

    def inner(a, b):
        return jnp.sum(a * b, axis=0, keepdims=True)

    mine[...] = jnp.concatenate(
        [inner(resid, precond), inner(precond, image), inner(image, again),
         inner(again, image_again), unit, jnp.zeros((3, COLS), F32)], axis=0,
    )

    def spread(source, slots, here, steps, sems):
        count = len(steps) + 1
        slots[here] = source[...]
        for step in steps:
            pltpu.make_async_remote_copy(
                source, slots.at[here], sems.at[0], sems.at[1],
                device_id=at(**step), device_id_type=MESH,
            ).start()
        rest = slots.at[pl.ds(0, count - 1)]
        pltpu.make_async_copy(rest, rest, sems.at[1]).wait()
        return combine(slots, count)

    def sent(slots, steps, sems):
        rest = slots.at[pl.ds(0, len(steps))]
        pltpu.make_async_copy(rest, rest, sems.at[0]).wait()

    row_steps = [dict(dz=dz, dc=dc) for dz, dc in ROW_STEPS]
    fan_steps = [dict(dy=dy, dx=dx) for dy, dx in FAN_STEPS]
    row_sum[...] = spread(mine, slots_a, zc, row_steps, sem_a)
    total = spread(row_sum, slots_b, y * GRP + grp, fan_steps, sem_b)
    row = lax.broadcasted_iota(I32, (8, COLS), 0)
    top = jnp.max(total[4:5], axis=1, keepdims=True)
    total = jnp.sum(weigh(total, total[4:5] / top, row), axis=1, keepdims=True)
    rz, pq, quq, uw = (total[i : i + 1] for i in range(4))
    alpha = rz / pq
    rz_next = alpha * alpha * quq - rz
    grown = 1.0 + rz_next / rz
    alpha_next = rz_next / (alpha * alpha * uw - grown * grown * pq)
    lam_out[:, 0, :] = (
        (alpha + alpha_next * grown) / top * precond
        - alpha_next * alpha / top * (unit / top) * again
    )
    sent(slots_a, row_steps, sem_a)
    sent(slots_b, fan_steps, sem_b)
    pltpu.make_async_copy(others, others, move_sems.at[0]).wait()


def per_device(gradients, moduli, diag_terms, counts, targets, compliance, neighbours, rhs):
    vmem = lambda shape, dtype=F32: pltpu.VMEM(shape, dtype)
    dma = pltpu.SemaphoreType.DMA
    lam, stiff = pl.pallas_call(
        kernel,
        out_shape=(
            pltpu.VMEM((N, 1, COLS), F32),
            pltpu.VMEM((N * N, 1, COLS), F32),
        ),
        in_specs=[pl.BlockSpec(memory_space=pltpu.HBM)] * 8,
        out_specs=[pl.BlockSpec(memory_space=pltpu.VMEM)] * 2,
        scratch_shapes=[
            vmem((9, N, ELEMS), BF16),
            vmem((9, ELEMS), BF16),
            vmem((N, ELEMS), BF16),
            vmem((1, SUB), I32),
            vmem((1, ELEMS), I32),
            vmem((1, COLS), I32),
            vmem((N, 1, COLS)),
            vmem((N * N, COLS)),
            vmem((N * N, COLS)),
            vmem((SLOT_ROWS, LANES_OF * ELEMS), BF16),
            vmem((2 * COLS, LANES_OF * ELEMS), BF16),
            vmem((2 * COLS, LANES_OF * ELEMS), BF16),
            vmem((SUB, ROWS_OF, COLS), I32),
            vmem((SUB, ROWS_OF, COLS), I32),
            vmem((96, COLS)),
            vmem((96, COLS)),
            vmem((8, COLS)),
            vmem((8, COLS)),
            vmem((ROW, 8, COLS)),
            vmem((COL * GRP, 8, COLS)),
            dma((8,)),
            pltpu.SemaphoreType.REGULAR((COL,)),
            dma((2,)),
            dma,
            dma((2,)),
            dma((2,)),
            dma((2,)),
            dma((2,)),
        ],
        compiler_params=pltpu.CompilerParams(
            collective_id=0, has_side_effects=True, vmem_limit_bytes=20 * 1024 * 1024
        ),
    )(
        *(
            pltpu.with_memory_space_constraint(operand, pltpu.HBM)
            for operand in (
                gradients[:, :, 0, :],
                moduli[:, 0, :],
                diag_terms[:, 0, :],
                counts[0],
                targets,
                compliance[:, 0, :],
                neighbours[0],
                rhs,
            )
        )
    )
    return lam, stiff


def solution(mesh):
    in_specs = (
        P(None, None, "grp", "sub"),
        P(None, "grp", "sub"),
        P(None, "grp", "sub"),
        P("grp", "sub", None),
        P("grp", "sub"),
        P(None, "grp", "sub"),
        P("grp", "sub", None),
        P(None, "grp", "sub"),
    )
    out_specs = (P(None, "grp", "sub"), P(None, "grp", "sub"))
    return jax.shard_map(
        per_device, mesh=mesh, in_specs=in_specs, out_specs=out_specs, check_vma=False
    )
```

```python
import jax
import jax.numpy as jnp
from jax import lax
from jax.experimental import pallas as pl
from jax.experimental.pallas import tpu as pltpu
from jax.sharding import PartitionSpec as P

MESH = pl.DeviceIdType.MESH
F32, BF16, I32 = jnp.float32, jnp.bfloat16, jnp.int32
N = 12
HALF = 7
ROW, COL, GRP = 16, 8, 4
SUB = ROW * COL
ELEMS = 512
COLS = 128
CAP = 12
WORDS = 42
LANES_OF = 3
ROWS_OF = CAP // LANES_OF
SLOT_ROWS = SUB * ROWS_OF


def hops(step, size):
    return min(step % size, -step % size)


ROW_STEPS = sorted(((z, c) for z in range(8) for c in range(2) if z or c), key=lambda s: -hops(s[0], 8))
FAN_STEPS = sorted(
    ((y, x) for y in range(COL) for x in range(GRP) if y or x),
    key=lambda s: -hops(s[0], COL) - hops(s[1], GRP),
)
FIRST_ROW = 5
ROW_ORDER = sorted(range(COL), key=lambda r: hops(r, COL))
COL_STEPS = sorted(range(1, COL), key=lambda s: -hops(s, COL))


def dot_nt(a, b):
    return lax.dot_general(a, b, (((1,), (1,)), ((), ())), preferred_element_type=F32)


def tangents(grads, mods, diag):
    sums = [None] * HALF
    for m in range(9):
        g = grads[m]
        weighted = g * mods[m : m + 1]
        wrapped = jnp.concatenate([g, g[:6]], axis=0)
        for d in range(HALF):
            rows = 6 if d == 6 else N
            term = weighted[:rows] * wrapped[d : d + rows]
            sums[d] = term if sums[d] is None else sums[d] + term
    sums[0] = sums[0] + diag
    return sums


def apply_half(k, v):
    twice = jnp.concatenate([v, v], axis=0)
    out = k[0] * v
    for d in range(1, 6):
        out = out + k[d] * twice[d : d + N]
        back = k[d] * v
        back = jnp.concatenate([back, back], axis=0)
        out = out + back[N - d : 2 * N - d]
    k6 = jnp.concatenate([k[6], k[6]], axis=0)
    return out + k6 * twice[6 : 6 + N]


def apply_full(k_ref, v):
    out = None
    for b in range(N):
        term = k_ref[b * N : (b + 1) * N, :] * v[b : b + 1]
        out = term if out is None else out + term
    return out


def combine(rows):
    lane = lax.broadcasted_iota(I32, rows.shape, 1)
    units = jnp.sum(jnp.where(lane == 4, rows, 0.0), axis=1, keepdims=True)
    units = jnp.broadcast_to(units, rows.shape)
    top = jnp.max(units, axis=0, keepdims=True)
    ratio = units / top
    square = ratio * ratio
    power = jnp.where(lane == 1, ratio, jnp.where(lane == 2, square, square * ratio))
    total = jnp.sum(rows * jnp.where(lane == 0, 1.0, power), axis=0, keepdims=True)
    return jnp.where(lane[:1] < 4, total, top)


def kernel(
    grads, mods, diag, counts, targets, comp, neigh, rhs,
    lam_out, stiff_out,
    g_v, m_v, d_v, c_v, t_v, n_v, r_v, own_c, near_c,
    sel, bytes_of, send, recv, half_own, half_near,
    mine, row_sum, slots_a, slots_b,
    in_sem, row_sems, comp_sems, sent_sem, arrived, half_sems, sem_a, sem_b,
):
    me, grp = lax.axis_index("sub"), lax.axis_index("grp")
    y, zc = me // ROW, me % ROW
    behind = (me, (grp + GRP - 1) % GRP)

    z, core = zc // 2, zc % 2

    def at(dy=0, dz=0, dc=0, dx=0):
        row = y if dy == 0 else (y + dy) % COL
        col = z if dz == 0 else (z + dz) % 8
        side = core if dc == 0 else 1 - core
        return row * ROW + col * 2 + side, (grp if dx == 0 else (grp + dx) % GRP)

    barrier = pltpu.get_barrier_semaphore()

    def greet(device):
        pl.semaphore_signal(barrier, inc=1, device_id=device, device_id_type=MESH)

    steps = [(hops(dz, 8), dict(dz=dz, dc=dc)) for dz, dc in ROW_STEPS]
    steps += [(hops(dy, COL), dict(dy=dy)) for dy in COL_STEPS]
    steps = [step for _, step in sorted(steps, key=lambda s: -s[0])]
    for step in steps[:9]:
        greet(at(**step))
    loads = [(counts, c_v), (grads, g_v), (mods, m_v), (diag, d_v), (targets, t_v),
             (comp, own_c), (neigh, n_v), (rhs, r_v)]
    loads = [pltpu.make_async_copy(a, b, in_sem.at[i]) for i, (a, b) in enumerate(loads)]
    for copy in loads:
        copy.start()
    for step in steps[9:]:
        greet(at(**step))
    for dx in (2, 1, 3):
        greet(at(dx=dx))

    loads[0].wait()
    line = lax.broadcasted_iota(I32, (SLOT_ROWS, COLS), 0)
    lane = lax.broadcasted_iota(I32, (SLOT_ROWS, COLS), 1)
    per_peer = jnp.broadcast_to(c_v[...].astype(F32), (COLS, SUB)).astype(BF16)
    first = dot_nt((lane < line // ROWS_OF).astype(F32).astype(BF16), per_peer)
    listed = dot_nt((lane == line // ROWS_OF).astype(F32).astype(BF16), per_peer)
    place = ((line % ROWS_OF) * LANES_OF).astype(F32)
    lane_f = lane.astype(F32)
    for j in range(LANES_OF):
        wanted = jnp.where(place + j < listed, first + place + j, -1.0)
        for t in range(ELEMS // COLS):
            hit = jnp.where(wanted == lane_f + t * COLS, 1.0, 0.0)
            sel[j, :, t * COLS : (t + 1) * COLS] = hit.astype(BF16)

    for copy in loads[1:5]:
        copy.wait()
    bytes_of[...] = jnp.zeros_like(bytes_of)
    mods_f = m_v[...].astype(F32)
    for t in range(ELEMS // COLS):
        here = pl.ds(t * COLS, COLS)
        tile = tangents(
            [g_v[m, :, here].astype(F32) for m in range(9)],
            mods_f[:, t * COLS : (t + 1) * COLS],
            d_v[:, here].astype(F32),
        )
        biggest = jnp.max(tile[0], axis=0, keepdims=True)
        step = (biggest * 1.01).astype(BF16).astype(F32)
        scale = 32768.0 / step
        meta = jnp.concatenate(
            [t_v[:, here].astype(F32), step * 512.0, jnp.zeros((4, COLS), F32)], axis=0
        )
        high = [jnp.floor(tile[d] * scale + 0.5) for d in (0, 2, 4, 6)]
        low = [jnp.floor(tile[d] * scale + 0.5) for d in (1, 3, 5)] + [meta]
        for half, values in enumerate((high, low)):
            values = jnp.concatenate(values, axis=0)
            upper = jnp.floor(values * (1.0 / 256.0)) * 256.0
            both = jnp.concatenate([upper, values - upper], axis=0)
            bytes_of[half * COLS : half * COLS + 2 * WORDS, here] = both.astype(BF16)

    lane = lax.broadcasted_iota(I32, (COLS, COLS), 1)
    for c in range(4):
        rows = pl.ds(c * COLS, COLS)
        words = None
        for j in range(LANES_OF):
            found = dot_nt(sel[j, rows, :], bytes_of[...])
            high, low = (
                (half + pltpu.roll(half, COLS - WORDS, 1)).astype(I32)
                for half in (found[:, :COLS], found[:, COLS:])
            )
            word = jnp.where(lane < WORDS, (high << 16) | (low & 0xFFFF), 0)
            words = word if j == 0 else words | pltpu.roll(word, j * WORDS, 1)
        send[pl.ds(c * 32, 32)] = words.reshape(32, ROWS_OF, COLS)

    pl.semaphore_wait(barrier, ROW + COL + GRP - 3)
    for dy in COL_STEPS:
        pl.semaphore_signal(
            row_sems.at[y], inc=1, device_id=at(dy=dy), device_id_type=MESH
        )
    for copy in loads[5:]:
        copy.wait()
    comp_copy = pltpu.make_async_remote_copy(
        own_c, near_c, comp_sems.at[0], comp_sems.at[1], device_id=behind, device_id_type=MESH
    )
    comp_copy.start()

    shifted = (y + FIRST_ROW) % COL
    slot, group = shifted * ROW + zc, shifted // (COL // 2)
    pltpu.make_async_copy(send.at[me], recv.at[slot], arrived.at[group]).start()

    def post(device):
        pltpu.make_async_remote_copy(
            send.at[device[0]], recv.at[slot], sent_sem, arrived.at[group],
            device_id=device, device_id_type=MESH,
        ).start()

    for dy in COL_STEPS:
        post(at(dy=dy))
    for dz, dc in ROW_STEPS:
        post(at(dz=dz, dc=dc))
    for dy in reversed(COL_STEPS):
        pl.semaphore_wait(row_sems.at[(y + dy) % COL], 1)
        for dz, dc in ROW_STEPS:
            post(at(dy, dz, dc))

    comp_copy.wait()
    facing = jnp.broadcast_to(n_v[...], (8, COLS))

    def moved(block):
        rows = block.shape[0]
        if rows % 8:
            block = jnp.concatenate([block, jnp.zeros((8 - rows % 8, COLS), F32)], axis=0)
        parts = [
            jnp.take_along_axis(block[i : i + 8], facing, axis=1)
            for i in range(0, block.shape[0], 8)
        ]
        return jnp.concatenate(parts, axis=0)[:rows]

    both_c = own_c[...] + moved(near_c[...])
    unit = both_c[0:1]
    for a in range(1, N):
        unit = jnp.maximum(unit, both_c[a * (N + 1) : a * (N + 1) + 1])
    unit = jnp.max(unit, axis=1, keepdims=True)
    own_c[...] = both_c / unit

    lane = lax.broadcasted_iota(I32, (COLS, COLS), 1)
    patch = lax.broadcasted_iota(I32, (COLS, SLOT_ROWS // 2), 0).astype(F32)
    sums = [jnp.zeros((COLS, COLS), F32)] * 2
    for group in (1, 0):
        block = recv.at[pl.ds(group * (SUB // 2), SUB // 2)]
        pltpu.make_async_copy(block, block, arrived.at[group]).wait()
        words = block[...].reshape(SLOT_ROWS // 2, COLS)
        high = words >> 16
        low = (words << 16) >> 16
        pieces = [high >> 8, high & 255, low >> 8, low & 255]
        pieces = jnp.concatenate([p.astype(F32).astype(BF16) for p in pieces], axis=1)
        meta = low.astype(F32).T
        for j in range(LANES_OF):
            target = meta[j * WORDS + 36 : j * WORDS + 37]
            code = meta[j * WORDS + 37 : j * WORDS + 38]
            step = jnp.where(code < 0.0, code + 65536.0, code) * (1.0 / 512.0)
            hit = jnp.where(patch == target, step, 0.0).astype(BF16)
            part = jnp.dot(hit, pieces, preferred_element_type=F32)
            here = (lane >= j * WORDS) & (lane < (j + 1) * WORDS)
            for half in range(2):
                upper = part[:, half * 256 : half * 256 + 128]
                lower = part[:, half * 256 + 128 : half * 256 + 256]
                sums[half] = sums[half] + jnp.where(here, upper * 256.0 + lower, 0.0)
    for half in range(2):
        turned = sums[half].T * (1.0 / 32768.0)
        folded = turned[:WORDS] + turned[WORDS : 2 * WORDS] + turned[2 * WORDS : 3 * WORDS]
        half_own[half * 48 : half * 48 + 48, :] = jnp.concatenate(
            [folded, jnp.zeros((6, COLS), F32)], axis=0
        )
    half_copy = pltpu.make_async_remote_copy(
        half_own, half_near, half_sems.at[0], half_sems.at[1], device_id=behind, device_id_type=MESH
    )
    half_copy.start()
    start_of = [0, 48, 12, 60, 24, 72, 36]
    for a in range(N):
        for b in range(N):
            d = (b - a) % N
            source = start_of[d] + a % (6 if d == 6 else N) if d < HALF else start_of[N - d] + b
            stiff_out[a * N + b] = half_own[source : source + 1, :]
    half_copy.wait()

    both = half_own[...] + moved(half_near[...])
    k = [both[s : s + (6 if d == 6 else N)] for d, s in enumerate(start_of)]
    k[0] = k[0] + 2.0

    resid = r_v[:, 0, :]
    precond = apply_half(k, resid)
    image = apply_full(own_c, precond)
    again = apply_half(k, image)
    image_again = apply_full(own_c, again)

    def inner(a, b):
        return jnp.sum(a * b, axis=0, keepdims=True)

    totals = jnp.concatenate(
        [inner(resid, precond), inner(precond, image), inner(image, again),
         inner(again, image_again)], axis=0,
    )
    totals = jnp.sum(totals, axis=1, keepdims=True)
    lane = lax.broadcasted_iota(I32, (1, COLS), 1)
    line = jnp.broadcast_to(unit, (1, COLS))
    for i in range(4):
        line = jnp.where(lane == i, totals[i : i + 1], line)
    mine[...] = line

    def spread(source, slots, here, steps, sems):
        count = len(steps) + 1
        slots[here] = source[...]
        for step in steps:
            pltpu.make_async_remote_copy(
                source, slots.at[here], sems.at[0], sems.at[1],
                device_id=at(**step), device_id_type=MESH,
            ).start()
        rest = slots.at[pl.ds(0, count - 1)]
        pltpu.make_async_copy(rest, rest, sems.at[1]).wait()
        return combine(slots[:, 0, :])

    def sent(slots, steps, sems):
        rest = slots.at[pl.ds(0, len(steps))]
        pltpu.make_async_copy(rest, rest, sems.at[0]).wait()

    row_steps = [dict(dz=dz, dc=dc) for dz, dc in ROW_STEPS]
    fan_steps = [dict(dy=dy, dx=dx) for dy, dx in FAN_STEPS]
    row_sum[...] = spread(mine, slots_a, zc, row_steps, sem_a)
    total = spread(row_sum, slots_b, y * GRP + grp, fan_steps, sem_b)
    rz, pq, quq, uw, top = (
        jnp.sum(jnp.where(lane == i, total, 0.0), axis=1, keepdims=True) for i in range(5)
    )
    alpha = rz / pq
    rz_next = alpha * alpha * quq - rz
    grown = 1.0 + rz_next / rz
    alpha_next = rz_next / (alpha * alpha * uw - grown * grown * pq)
    lam_out[:, 0, :] = (
        (alpha + alpha_next * grown) / top * precond
        - alpha_next * alpha / top * (unit / top) * again
    )
    sent(slots_a, row_steps, sem_a)
    sent(slots_b, fan_steps, sem_b)
    others = recv.at[pl.ds(0, SUB - 1)]
    pltpu.make_async_copy(others, others, sent_sem).wait()


def per_device(gradients, moduli, diag_terms, counts, targets, compliance, neighbours, rhs):
    vmem = lambda shape, dtype=F32: pltpu.VMEM(shape, dtype)
    dma = pltpu.SemaphoreType.DMA
    lam, stiff = pl.pallas_call(
        kernel,
        out_shape=(
            pltpu.VMEM((N, 1, COLS), F32),
            pltpu.VMEM((N * N, 1, COLS), F32),
        ),
        in_specs=[pl.BlockSpec(memory_space=pltpu.HBM)] * 8,
        out_specs=[pl.BlockSpec(memory_space=pltpu.VMEM)] * 2,
        scratch_shapes=[
            vmem((9, N, ELEMS), BF16),
            vmem((9, ELEMS), BF16),
            vmem((N, ELEMS), BF16),
            vmem((1, SUB), I32),
            vmem((1, ELEMS), I32),
            vmem((1, COLS), I32),
            vmem((N, 1, COLS)),
            vmem((N * N, COLS)),
            vmem((N * N, COLS)),
            vmem((LANES_OF, SLOT_ROWS, ELEMS), BF16),
            vmem((2 * COLS, ELEMS), BF16),
            vmem((SUB, ROWS_OF, COLS), I32),
            vmem((SUB, ROWS_OF, COLS), I32),
            vmem((96, COLS)),
            vmem((96, COLS)),
            vmem((1, COLS)),
            vmem((1, COLS)),
            vmem((ROW, 1, COLS)),
            vmem((COL * GRP, 1, COLS)),
            dma((8,)),
            pltpu.SemaphoreType.REGULAR((COL,)),
            dma((2,)),
            dma,
            dma((2,)),
            dma((2,)),
            dma((2,)),
            dma((2,)),
        ],
        compiler_params=pltpu.CompilerParams(
            collective_id=0, has_side_effects=True, vmem_limit_bytes=20 * 1024 * 1024
        ),
    )(
        *(
            pltpu.with_memory_space_constraint(operand, pltpu.HBM)
            for operand in (
                gradients[:, :, 0, :],
                moduli[:, 0, :],
                diag_terms[:, 0, :],
                counts[0],
                targets,
                compliance[:, 0, :],
                neighbours[0],
                rhs,
            )
        )
    )
    return pl.pallas_call(
        place,
        out_shape=(
            jax.ShapeDtypeStruct((N, 1, COLS), F32),
            jax.ShapeDtypeStruct((N * N, 1, COLS), F32),
        ),
        in_specs=[pl.BlockSpec(memory_space=pltpu.VMEM)] * 2,
        out_specs=[pl.BlockSpec(memory_space=pl.ANY)] * 2,
        scratch_shapes=[dma((2,))],
        compiler_params=pltpu.CompilerParams(vmem_limit_bytes=20 * 1024 * 1024),
    )(
        pltpu.with_memory_space_constraint(lam, pltpu.VMEM),
        pltpu.with_memory_space_constraint(stiff, pltpu.VMEM),
    )


def place(lam, stiff, lam_out, stiff_out, sems):
    copies = [
        pltpu.make_async_copy(stiff, stiff_out, sems.at[0]),
        pltpu.make_async_copy(lam, lam_out, sems.at[1]),
    ]
    for copy in copies:
        copy.start()
    for copy in copies:
        copy.wait()


def solution(mesh):
    in_specs = (
        P(None, None, "grp", "sub"),
        P(None, "grp", "sub"),
        P(None, "grp", "sub"),
        P("grp", "sub", None),
        P("grp", "sub"),
        P(None, "grp", "sub"),
        P("grp", "sub", None),
        P(None, "grp", "sub"),
    )
    out_specs = (P(None, "grp", "sub"), P(None, "grp", "sub"))
    return jax.shard_map(
        per_device, mesh=mesh, in_specs=in_specs, out_specs=out_specs, check_vma=False
    )
```

```python
import jax
import jax.numpy as jnp
from jax import lax
from jax.experimental import pallas as pl
from jax.experimental.pallas import tpu as pltpu
from jax.sharding import PartitionSpec as P

MESH = pl.DeviceIdType.MESH
F32, BF16, I32 = jnp.float32, jnp.bfloat16, jnp.int32
N = 12
HALF = 7
ROW, COL, GRP = 16, 8, 4
SUB = ROW * COL
ELEMS = 512
COLS = 128
CAP = 12
WORDS = 42
LANES_OF = 3
ROWS_OF = CAP // LANES_OF
SLOT_ROWS = SUB * ROWS_OF


def hops(step, size):
    return min(step % size, -step % size)


ROW_STEPS = sorted(((z, c) for z in range(8) for c in range(2) if z or c), key=lambda s: -hops(s[0], 8))
FAN_STEPS = sorted(
    ((y, x) for y in range(COL) for x in range(GRP) if y or x),
    key=lambda s: -hops(s[0], COL) - hops(s[1], GRP),
)
COL_STEPS = sorted(range(1, COL), key=lambda s: -hops(s, COL))
SERVED = [0] + COL_STEPS[::-1]
EARLY = 6


def dot_nt(a, b):
    return lax.dot_general(a, b, (((1,), (1,)), ((), ())), preferred_element_type=F32)


def tangents(grads, mods, diag):
    sums = [None] * HALF
    for m in range(9):
        g = grads[m]
        weighted = g * mods[m : m + 1]
        wrapped = jnp.concatenate([g, g[:6]], axis=0)
        for d in range(HALF):
            rows = 6 if d == 6 else N
            term = weighted[:rows] * wrapped[d : d + rows]
            sums[d] = term if sums[d] is None else sums[d] + term
    sums[0] = sums[0] + diag
    return sums


def apply_half(k, v):
    twice = jnp.concatenate([v, v], axis=0)
    out = k[0] * v
    for d in range(1, 6):
        out = out + k[d] * twice[d : d + N]
        back = k[d] * v
        back = jnp.concatenate([back, back], axis=0)
        out = out + back[N - d : 2 * N - d]
    k6 = jnp.concatenate([k[6], k[6]], axis=0)
    return out + k6 * twice[6 : 6 + N]


def apply_full(k_ref, v):
    out = None
    for b in range(N):
        term = k_ref[b * N : (b + 1) * N, :] * v[b : b + 1]
        out = term if out is None else out + term
    return out


def combine(rows):
    lane = lax.broadcasted_iota(I32, rows.shape, 1)
    units = jnp.sum(jnp.where(lane == 4, rows, 0.0), axis=1, keepdims=True)
    units = jnp.broadcast_to(units, rows.shape)
    top = jnp.max(units, axis=0, keepdims=True)
    ratio = units / top
    square = ratio * ratio
    power = jnp.where(lane == 1, ratio, jnp.where(lane == 2, square, square * ratio))
    total = jnp.sum(rows * jnp.where(lane == 0, 1.0, power), axis=0, keepdims=True)
    return jnp.where(lane[:1] < 4, total, top)


def kernel(
    grads, mods, diag, counts, targets, comp, neigh, rhs,
    lam_out, stiff_out,
    g_v, m_v, d_v, c_v, t_v, n_v, r_v, own_c, near_c,
    sel, bytes_of, send, recv, half_own, half_near,
    mine, row_sum, slots_a, slots_b,
    in_sem, row_sems, comp_sems, sent_sem, arrived, half_sems, sem_a, sem_b,
):
    me, grp = lax.axis_index("sub"), lax.axis_index("grp")
    y, zc = me // ROW, me % ROW
    behind = (me, (grp + GRP - 1) % GRP)

    z, core = zc // 2, zc % 2

    def at(dy=0, dz=0, dc=0, dx=0):
        row = y if dy == 0 else (y + dy) % COL
        col = z if dz == 0 else (z + dz) % 8
        side = core if dc == 0 else 1 - core
        return row * ROW + col * 2 + side, (grp if dx == 0 else (grp + dx) % GRP)

    barrier = pltpu.get_barrier_semaphore()

    def greet(device):
        pl.semaphore_signal(barrier, inc=1, device_id=device, device_id_type=MESH)

    steps = [(hops(dz, 8), dict(dz=dz, dc=dc)) for dz, dc in ROW_STEPS]
    steps += [(hops(dy, COL), dict(dy=dy)) for dy in COL_STEPS]
    steps = [step for _, step in sorted(steps, key=lambda s: -s[0])]
    for step in steps[:9]:
        greet(at(**step))
    loads = [(counts, c_v), (grads, g_v), (mods, m_v), (diag, d_v), (targets, t_v),
             (comp, own_c), (neigh, n_v), (rhs, r_v)]
    loads = [pltpu.make_async_copy(a, b, in_sem.at[i]) for i, (a, b) in enumerate(loads)]
    for copy in loads:
        copy.start()
    for step in steps[9:]:
        greet(at(**step))
    for dx in (2, 1, 3):
        greet(at(dx=dx))

    loads[0].wait()
    line = lax.broadcasted_iota(I32, (SLOT_ROWS, COLS), 0)
    lane = lax.broadcasted_iota(I32, (SLOT_ROWS, COLS), 1)
    per_peer = jnp.broadcast_to(c_v[...].astype(F32), (COLS, SUB)).astype(BF16)
    first = dot_nt((lane < line // ROWS_OF).astype(F32).astype(BF16), per_peer)
    listed = dot_nt((lane == line // ROWS_OF).astype(F32).astype(BF16), per_peer)
    place = ((line % ROWS_OF) * LANES_OF).astype(F32)
    lane_f = lane.astype(F32)
    for j in range(LANES_OF):
        wanted = jnp.where(place + j < listed, first + place + j, -1.0)
        for t in range(ELEMS // COLS):
            hit = jnp.where(wanted == lane_f + t * COLS, 1.0, 0.0)
            sel[j, :, t * COLS : (t + 1) * COLS] = hit.astype(BF16)

    for copy in loads[1:5]:
        copy.wait()
    bytes_of[...] = jnp.zeros_like(bytes_of)
    mods_f = m_v[...].astype(F32)
    for t in range(ELEMS // COLS):
        here = pl.ds(t * COLS, COLS)
        tile = tangents(
            [g_v[m, :, here].astype(F32) for m in range(9)],
            mods_f[:, t * COLS : (t + 1) * COLS],
            d_v[:, here].astype(F32),
        )
        biggest = jnp.max(tile[0], axis=0, keepdims=True)
        step = (biggest * 1.01).astype(BF16).astype(F32)
        scale = 32768.0 / step
        meta = jnp.concatenate(
            [t_v[:, here].astype(F32), step * 512.0, jnp.zeros((4, COLS), F32)], axis=0
        )
        high = [jnp.floor(tile[d] * scale + 0.5) for d in (0, 2, 4, 6)]
        low = [jnp.floor(tile[d] * scale + 0.5) for d in (1, 3, 5)] + [meta]
        for half, values in enumerate((high, low)):
            values = jnp.concatenate(values, axis=0)
            upper = jnp.floor(values * (1.0 / 256.0)) * 256.0
            both = jnp.concatenate([upper, values - upper], axis=0)
            bytes_of[half * COLS : half * COLS + 2 * WORDS, here] = both.astype(BF16)

    lane = lax.broadcasted_iota(I32, (COLS, COLS), 1)
    for c in range(4):
        rows = pl.ds(c * COLS, COLS)
        words = None
        for j in range(LANES_OF):
            found = dot_nt(sel[j, rows, :], bytes_of[...])
            high, low = (
                (half + pltpu.roll(half, COLS - WORDS, 1)).astype(I32)
                for half in (found[:, :COLS], found[:, COLS:])
            )
            word = jnp.where(lane < WORDS, (high << 16) | (low & 0xFFFF), 0)
            words = word if j == 0 else words | pltpu.roll(word, j * WORDS, 1)
        send[pl.ds(c * 32, 32)] = words.reshape(32, ROWS_OF, COLS)

    pl.semaphore_wait(barrier, ROW + COL + GRP - 3)
    for dy in COL_STEPS:
        pl.semaphore_signal(
            row_sems.at[y], inc=1, device_id=at(dy=dy), device_id_type=MESH
        )
    for copy in loads[5:]:
        copy.wait()
    comp_copy = pltpu.make_async_remote_copy(
        own_c, near_c, comp_sems.at[0], comp_sems.at[1], device_id=behind, device_id_type=MESH
    )
    comp_copy.start()

    pltpu.make_async_copy(send.at[me], recv.at[zc], arrived.at[0]).start()

    def post(dy, dz, dc):
        device, place = at(dy, dz, dc), SERVED.index(dy)
        pltpu.make_async_remote_copy(
            send.at[device[0]], recv.at[place * ROW + zc], sent_sem,
            arrived.at[0 if place < EARLY else 1], device_id=device, device_id_type=MESH,
        ).start()

    for dy in COL_STEPS:
        post(dy, 0, 0)
    for dz, dc in ROW_STEPS:
        post(0, dz, dc)
    for dy in SERVED[1:]:
        pl.semaphore_wait(row_sems.at[(y + dy) % COL], 1)
        for dz, dc in ROW_STEPS:
            post(dy, dz, dc)

    comp_copy.wait()
    facing = jnp.broadcast_to(n_v[...], (8, COLS))

    def moved(block):
        rows = block.shape[0]
        if rows % 8:
            block = jnp.concatenate([block, jnp.zeros((8 - rows % 8, COLS), F32)], axis=0)
        parts = [
            jnp.take_along_axis(block[i : i + 8], facing, axis=1)
            for i in range(0, block.shape[0], 8)
        ]
        return jnp.concatenate(parts, axis=0)[:rows]

    both_c = own_c[...] + moved(near_c[...])
    unit = both_c[0:1]
    for a in range(1, N):
        unit = jnp.maximum(unit, both_c[a * (N + 1) : a * (N + 1) + 1])
    unit = jnp.max(unit, axis=1, keepdims=True)
    own_c[...] = both_c / unit

    lane = lax.broadcasted_iota(I32, (COLS, COLS), 1)
    sums = [jnp.zeros((COLS, COLS), F32)] * 2
    for group, rows in enumerate((EARLY, COL - EARLY)):
        lines = rows * ROW * ROWS_OF
        block = recv.at[pl.ds(group * EARLY * ROW, rows * ROW)]
        pltpu.make_async_copy(block, block, arrived.at[group]).wait()
        words = block[...].reshape(lines, COLS)
        patch = lax.broadcasted_iota(I32, (COLS, lines), 0).astype(F32)
        high = words >> 16
        low = (words << 16) >> 16
        pieces = [high >> 8, high & 255, low >> 8, low & 255]
        pieces = jnp.concatenate([p.astype(F32).astype(BF16) for p in pieces], axis=1)
        meta = low.astype(F32).T
        for j in range(LANES_OF):
            target = meta[j * WORDS + 36 : j * WORDS + 37]
            code = meta[j * WORDS + 37 : j * WORDS + 38]
            step = jnp.where(code < 0.0, code + 65536.0, code) * (1.0 / 512.0)
            hit = jnp.where(patch == target, step, 0.0).astype(BF16)
            part = jnp.dot(hit, pieces, preferred_element_type=F32)
            here = (lane >= j * WORDS) & (lane < (j + 1) * WORDS)
            for half in range(2):
                upper = part[:, half * 256 : half * 256 + 128]
                lower = part[:, half * 256 + 128 : half * 256 + 256]
                sums[half] = sums[half] + jnp.where(here, upper * 256.0 + lower, 0.0)
    for half in range(2):
        turned = sums[half].T * (1.0 / 32768.0)
        folded = turned[:WORDS] + turned[WORDS : 2 * WORDS] + turned[2 * WORDS : 3 * WORDS]
        half_own[half * 48 : half * 48 + 48, :] = jnp.concatenate(
            [folded, jnp.zeros((6, COLS), F32)], axis=0
        )
    half_copy = pltpu.make_async_remote_copy(
        half_own, half_near, half_sems.at[0], half_sems.at[1], device_id=behind, device_id_type=MESH
    )
    half_copy.start()
    start_of = [0, 48, 12, 60, 24, 72, 36]
    for a in range(N):
        for b in range(N):
            d = (b - a) % N
            source = start_of[d] + a % (6 if d == 6 else N) if d < HALF else start_of[N - d] + b
            stiff_out[a * N + b] = half_own[source : source + 1, :]
    half_copy.wait()

    both = half_own[...] + moved(half_near[...])
    k = [both[s : s + (6 if d == 6 else N)] for d, s in enumerate(start_of)]
    k[0] = k[0] + 2.0

    resid = r_v[:, 0, :]
    precond = apply_half(k, resid)
    image = apply_full(own_c, precond)
    again = apply_half(k, image)
    image_again = apply_full(own_c, again)

    def inner(a, b):
        return jnp.sum(a * b, axis=0, keepdims=True)

    totals = jnp.concatenate(
        [inner(resid, precond), inner(precond, image), inner(image, again),
         inner(again, image_again)], axis=0,
    )
    totals = jnp.sum(totals, axis=1, keepdims=True)
    lane = lax.broadcasted_iota(I32, (1, COLS), 1)
    line = jnp.broadcast_to(unit, (1, COLS))
    for i in range(4):
        line = jnp.where(lane == i, totals[i : i + 1], line)
    mine[...] = line

    def spread(source, slots, here, steps, sems):
        count = len(steps) + 1
        slots[here] = source[...]
        for step in steps:
            pltpu.make_async_remote_copy(
                source, slots.at[here], sems.at[0], sems.at[1],
                device_id=at(**step), device_id_type=MESH,
            ).start()
        rest = slots.at[pl.ds(0, count - 1)]
        pltpu.make_async_copy(rest, rest, sems.at[1]).wait()
        return combine(slots[:, 0, :])

    def sent(slots, steps, sems):
        rest = slots.at[pl.ds(0, len(steps))]
        pltpu.make_async_copy(rest, rest, sems.at[0]).wait()

    row_steps = [dict(dz=dz, dc=dc) for dz, dc in ROW_STEPS]
    fan_steps = [dict(dy=dy, dx=dx) for dy, dx in FAN_STEPS]
    row_sum[...] = spread(mine, slots_a, zc, row_steps, sem_a)
    total = spread(row_sum, slots_b, y * GRP + grp, fan_steps, sem_b)
    rz, pq, quq, uw, top = (
        jnp.sum(jnp.where(lane == i, total, 0.0), axis=1, keepdims=True) for i in range(5)
    )
    alpha = rz / pq
    rz_next = alpha * alpha * quq - rz
    grown = 1.0 + rz_next / rz
    alpha_next = rz_next / (alpha * alpha * uw - grown * grown * pq)
    lam_out[:, 0, :] = (
        (alpha + alpha_next * grown) / top * precond
        - alpha_next * alpha / top * (unit / top) * again
    )
    sent(slots_a, row_steps, sem_a)
    sent(slots_b, fan_steps, sem_b)
    others = recv.at[pl.ds(0, SUB - 1)]
    pltpu.make_async_copy(others, others, sent_sem).wait()


def per_device(gradients, moduli, diag_terms, counts, targets, compliance, neighbours, rhs):
    vmem = lambda shape, dtype=F32: pltpu.VMEM(shape, dtype)
    dma = pltpu.SemaphoreType.DMA
    lam, stiff = pl.pallas_call(
        kernel,
        out_shape=(
            pltpu.VMEM((N, 1, COLS), F32),
            pltpu.VMEM((N * N, 1, COLS), F32),
        ),
        in_specs=[pl.BlockSpec(memory_space=pltpu.HBM)] * 8,
        out_specs=[pl.BlockSpec(memory_space=pltpu.VMEM)] * 2,
        scratch_shapes=[
            vmem((9, N, ELEMS), BF16),
            vmem((9, ELEMS), BF16),
            vmem((N, ELEMS), BF16),
            vmem((1, SUB), I32),
            vmem((1, ELEMS), I32),
            vmem((1, COLS), I32),
            vmem((N, 1, COLS)),
            vmem((N * N, COLS)),
            vmem((N * N, COLS)),
            vmem((LANES_OF, SLOT_ROWS, ELEMS), BF16),
            vmem((2 * COLS, ELEMS), BF16),
            vmem((SUB, ROWS_OF, COLS), I32),
            vmem((SUB, ROWS_OF, COLS), I32),
            vmem((96, COLS)),
            vmem((96, COLS)),
            vmem((1, COLS)),
            vmem((1, COLS)),
            vmem((ROW, 1, COLS)),
            vmem((COL * GRP, 1, COLS)),
            dma((8,)),
            pltpu.SemaphoreType.REGULAR((COL,)),
            dma((2,)),
            dma,
            dma((2,)),
            dma((2,)),
            dma((2,)),
            dma((2,)),
        ],
        compiler_params=pltpu.CompilerParams(
            collective_id=0, has_side_effects=True, vmem_limit_bytes=20 * 1024 * 1024
        ),
    )(
        *(
            pltpu.with_memory_space_constraint(operand, pltpu.HBM)
            for operand in (
                gradients[:, :, 0, :],
                moduli[:, 0, :],
                diag_terms[:, 0, :],
                counts[0],
                targets,
                compliance[:, 0, :],
                neighbours[0],
                rhs,
            )
        )
    )
    return pl.pallas_call(
        place,
        out_shape=(
            jax.ShapeDtypeStruct((N, 1, COLS), F32),
            jax.ShapeDtypeStruct((N * N, 1, COLS), F32),
        ),
        in_specs=[pl.BlockSpec(memory_space=pltpu.VMEM)] * 2,
        out_specs=[pl.BlockSpec(memory_space=pl.ANY)] * 2,
        scratch_shapes=[dma((2,))],
        compiler_params=pltpu.CompilerParams(vmem_limit_bytes=20 * 1024 * 1024),
    )(
        pltpu.with_memory_space_constraint(lam, pltpu.VMEM),
        pltpu.with_memory_space_constraint(stiff, pltpu.VMEM),
    )


def place(lam, stiff, lam_out, stiff_out, sems):
    copies = [
        pltpu.make_async_copy(stiff, stiff_out, sems.at[0]),
        pltpu.make_async_copy(lam, lam_out, sems.at[1]),
    ]
    for copy in copies:
        copy.start()
    for copy in copies:
        copy.wait()


def solution(mesh):
    in_specs = (
        P(None, None, "grp", "sub"),
        P(None, "grp", "sub"),
        P(None, "grp", "sub"),
        P("grp", "sub", None),
        P("grp", "sub"),
        P(None, "grp", "sub"),
        P("grp", "sub", None),
        P(None, "grp", "sub"),
    )
    out_specs = (P(None, "grp", "sub"), P(None, "grp", "sub"))
    return jax.shard_map(
        per_device, mesh=mesh, in_specs=in_specs, out_specs=out_specs, check_vma=False
    )
```

```python
import jax
import jax.numpy as jnp
from jax import lax
from jax.experimental import pallas as pl
from jax.experimental.pallas import tpu as pltpu
from jax.sharding import PartitionSpec as P

MESH = pl.DeviceIdType.MESH
F32, BF16, I32 = jnp.float32, jnp.bfloat16, jnp.int32
N = 12
HALF = 7
ROW, COL, GRP = 16, 8, 4
SUB = ROW * COL
ELEMS = 512
COLS = 128
CAP = 12
WORDS = 42
LANES_OF = 3
ROWS_OF = CAP // LANES_OF
SLOT_ROWS = SUB * ROWS_OF


def hops(step, size):
    return min(step % size, -step % size)


ROW_STEPS = sorted(((z, c) for z in range(8) for c in range(2) if z or c), key=lambda s: -hops(s[0], 8))
FAN_STEPS = sorted(
    ((y, x) for y in range(COL) for x in range(GRP) if y or x),
    key=lambda s: -hops(s[0], COL) - hops(s[1], GRP),
)
COL_STEPS = sorted(range(1, COL), key=lambda s: -hops(s, COL))
SERVED = [0] + COL_STEPS[::-1]
EARLY = 6


def dot_nt(a, b):
    return lax.dot_general(a, b, (((1,), (1,)), ((), ())), preferred_element_type=F32)


def tangents(grads, mods, diag):
    sums = [None] * HALF
    for m in range(9):
        g = grads[m]
        weighted = g * mods[m : m + 1]
        wrapped = jnp.concatenate([g, g[:6]], axis=0)
        for d in range(HALF):
            rows = 6 if d == 6 else N
            term = weighted[:rows] * wrapped[d : d + rows]
            sums[d] = term if sums[d] is None else sums[d] + term
    sums[0] = sums[0] + diag
    return sums


def apply_half(k, v):
    twice = jnp.concatenate([v, v], axis=0)
    out = k[0] * v
    for d in range(1, 6):
        out = out + k[d] * twice[d : d + N]
        back = k[d] * v
        back = jnp.concatenate([back, back], axis=0)
        out = out + back[N - d : 2 * N - d]
    k6 = jnp.concatenate([k[6], k[6]], axis=0)
    return out + k6 * twice[6 : 6 + N]


def apply_full(k_ref, v):
    out = None
    for b in range(N):
        term = k_ref[b * N : (b + 1) * N, :] * v[b : b + 1]
        out = term if out is None else out + term
    return out


def combine(rows):
    lane = lax.broadcasted_iota(I32, rows.shape, 1)
    units = jnp.sum(jnp.where(lane == 4, rows, 0.0), axis=1, keepdims=True)
    units = jnp.broadcast_to(units, rows.shape)
    top = jnp.max(units, axis=0, keepdims=True)
    ratio = units / top
    square = ratio * ratio
    power = jnp.where(lane == 1, ratio, jnp.where(lane == 2, square, square * ratio))
    total = jnp.sum(rows * jnp.where(lane == 0, 1.0, power), axis=0, keepdims=True)
    return jnp.where(lane[:1] < 4, total, top)


def kernel(
    grads, mods, diag, counts, targets, comp, neigh, rhs,
    lam_out, stiff_out,
    g_v, m_v, d_v, c_v, t_v, n_v, r_v, own_c, near_c,
    sel, bytes_of, send, recv, half_own, half_near,
    mine, row_sum, slots_a, slots_b,
    in_sem, row_sems, comp_sems, sent_sem, arrived, half_sems, sem_a, sem_b,
):
    me, grp = lax.axis_index("sub"), lax.axis_index("grp")
    y, zc = me // ROW, me % ROW
    behind = (me, (grp + GRP - 1) % GRP)

    z, core = zc // 2, zc % 2

    def at(dy=0, dz=0, dc=0, dx=0):
        row = y if dy == 0 else (y + dy) % COL
        col = z if dz == 0 else (z + dz) % 8
        side = core if dc == 0 else 1 - core
        return row * ROW + col * 2 + side, (grp if dx == 0 else (grp + dx) % GRP)

    barrier = pltpu.get_barrier_semaphore()

    def greet(device):
        pl.semaphore_signal(barrier, inc=1, device_id=device, device_id_type=MESH)

    steps = [(hops(dz, 8), dict(dz=dz, dc=dc)) for dz, dc in ROW_STEPS]
    steps += [(hops(dy, COL), dict(dy=dy)) for dy in COL_STEPS]
    steps = [step for _, step in sorted(steps, key=lambda s: -s[0])]
    for step in steps[:9]:
        greet(at(**step))
    loads = [(counts, c_v), (grads, g_v), (mods, m_v), (diag, d_v), (targets, t_v),
             (comp, own_c), (neigh, n_v), (rhs, r_v)]
    loads = [pltpu.make_async_copy(a, b, in_sem.at[i]) for i, (a, b) in enumerate(loads)]
    for copy in loads:
        copy.start()
    for step in steps[9:]:
        greet(at(**step))
    for dx in (2, 1, 3):
        greet(at(dx=dx))

    loads[0].wait()
    line = lax.broadcasted_iota(I32, (SLOT_ROWS, COLS), 0)
    lane = lax.broadcasted_iota(I32, (SLOT_ROWS, COLS), 1)
    per_peer = jnp.broadcast_to(c_v[...].astype(F32), (COLS, SUB)).astype(BF16)
    first = dot_nt((lane < line // ROWS_OF).astype(F32).astype(BF16), per_peer)
    listed = dot_nt((lane == line // ROWS_OF).astype(F32).astype(BF16), per_peer)
    place = ((line % ROWS_OF) * LANES_OF).astype(F32)
    lane_f = lane.astype(F32)
    for j in range(LANES_OF):
        wanted = jnp.where(place + j < listed, first + place + j, -1.0)
        for t in range(ELEMS // COLS):
            hit = jnp.where(wanted == lane_f + t * COLS, 1.0, 0.0)
            sel[j, :, t * COLS : (t + 1) * COLS] = hit.astype(BF16)

    for copy in loads[1:5]:
        copy.wait()
    bytes_of[...] = jnp.zeros_like(bytes_of)
    mods_f = m_v[...].astype(F32)
    for t in range(ELEMS // COLS):
        here = pl.ds(t * COLS, COLS)
        tile = tangents(
            [g_v[m, :, here].astype(F32) for m in range(9)],
            mods_f[:, t * COLS : (t + 1) * COLS],
            d_v[:, here].astype(F32),
        )
        biggest = jnp.max(tile[0], axis=0, keepdims=True)
        step = (biggest * 1.01).astype(BF16).astype(F32)
        scale = 32768.0 / step
        meta = jnp.concatenate(
            [t_v[:, here].astype(F32), step * 512.0, jnp.zeros((4, COLS), F32)], axis=0
        )
        high = [jnp.floor(tile[d] * scale + 0.5) for d in (0, 2, 4, 6)]
        low = [jnp.floor(tile[d] * scale + 0.5) for d in (1, 3, 5)] + [meta]
        for half, values in enumerate((high, low)):
            values = jnp.concatenate(values, axis=0)
            upper = jnp.floor(values * (1.0 / 256.0)) * 256.0
            both = jnp.concatenate([upper, values - upper], axis=0)
            bytes_of[half * COLS : half * COLS + 2 * WORDS, here] = both.astype(BF16)

    lane = lax.broadcasted_iota(I32, (COLS, COLS), 1)
    for c in range(4):
        rows = pl.ds(c * COLS, COLS)
        words = None
        for j in range(LANES_OF):
            found = dot_nt(sel[j, rows, :], bytes_of[...])
            high, low = (
                (half + pltpu.roll(half, COLS - WORDS, 1)).astype(I32)
                for half in (found[:, :COLS], found[:, COLS:])
            )
            word = jnp.where(lane < WORDS, (high << 16) | (low & 0xFFFF), 0)
            words = word if j == 0 else words | pltpu.roll(word, j * WORDS, 1)
        send[pl.ds(c * 32, 32)] = words.reshape(32, ROWS_OF, COLS)

    pl.semaphore_wait(barrier, ROW + COL + GRP - 3)
    for dy in COL_STEPS:
        pl.semaphore_signal(
            row_sems.at[y], inc=1, device_id=at(dy=dy), device_id_type=MESH
        )
    for copy in loads[5:]:
        copy.wait()
    comp_copy = pltpu.make_async_remote_copy(
        own_c, near_c, comp_sems.at[0], comp_sems.at[1], device_id=behind, device_id_type=MESH
    )
    comp_copy.start()

    pltpu.make_async_copy(send.at[me], recv.at[zc], arrived.at[0]).start()

    def post(dy, dz, dc):
        device, place = at(dy, dz, dc), SERVED.index(dy)
        pltpu.make_async_remote_copy(
            send.at[device[0]], recv.at[place * ROW + zc], sent_sem,
            arrived.at[0 if place < EARLY else 1], device_id=device, device_id_type=MESH,
        ).start()

    for dy in COL_STEPS:
        post(dy, 0, 0)
    for dz, dc in ROW_STEPS:
        post(0, dz, dc)
    for dy in SERVED[1:EARLY]:
        pl.semaphore_wait(row_sems.at[(y + dy) % COL], 1)
        for dz, dc in ROW_STEPS:
            post(dy, dz, dc)
    for dy in SERVED[EARLY:]:
        pl.semaphore_wait(row_sems.at[(y + dy) % COL], 1)
    for dz, dc in ROW_STEPS:
        for dy in SERVED[:EARLY - 1:-1]:
            post(dy, dz, dc)

    comp_copy.wait()
    facing = jnp.broadcast_to(n_v[...], (8, COLS))

    def moved(block):
        rows = block.shape[0]
        if rows % 8:
            block = jnp.concatenate([block, jnp.zeros((8 - rows % 8, COLS), F32)], axis=0)
        parts = [
            jnp.take_along_axis(block[i : i + 8], facing, axis=1)
            for i in range(0, block.shape[0], 8)
        ]
        return jnp.concatenate(parts, axis=0)[:rows]

    both_c = own_c[...] + moved(near_c[...])
    unit = both_c[0:1]
    for a in range(1, N):
        unit = jnp.maximum(unit, both_c[a * (N + 1) : a * (N + 1) + 1])
    unit = jnp.max(unit, axis=1, keepdims=True)
    own_c[...] = both_c / unit

    lane = lax.broadcasted_iota(I32, (COLS, COLS), 1)
    sums = [jnp.zeros((COLS, COLS), F32)] * 2
    for group, rows in enumerate((EARLY, COL - EARLY)):
        lines = rows * ROW * ROWS_OF
        block = recv.at[pl.ds(group * EARLY * ROW, rows * ROW)]
        pltpu.make_async_copy(block, block, arrived.at[group]).wait()
        words = block[...].reshape(lines, COLS)
        patch = lax.broadcasted_iota(I32, (COLS, lines), 0).astype(F32)
        high = words >> 16
        low = (words << 16) >> 16
        pieces = [high >> 8, high & 255, low >> 8, low & 255]
        pieces = jnp.concatenate([p.astype(F32).astype(BF16) for p in pieces], axis=1)
        meta = low.astype(F32).T
        for j in range(LANES_OF):
            target = meta[j * WORDS + 36 : j * WORDS + 37]
            code = meta[j * WORDS + 37 : j * WORDS + 38]
            step = jnp.where(code < 0.0, code + 65536.0, code) * (1.0 / 512.0)
            hit = jnp.where(patch == target, step, 0.0).astype(BF16)
            part = jnp.dot(hit, pieces, preferred_element_type=F32)
            here = (lane >= j * WORDS) & (lane < (j + 1) * WORDS)
            for half in range(2):
                upper = part[:, half * 256 : half * 256 + 128]
                lower = part[:, half * 256 + 128 : half * 256 + 256]
                sums[half] = sums[half] + jnp.where(here, upper * 256.0 + lower, 0.0)
    for half in range(2):
        turned = sums[half].T * (1.0 / 32768.0)
        folded = turned[:WORDS] + turned[WORDS : 2 * WORDS] + turned[2 * WORDS : 3 * WORDS]
        half_own[half * 48 : half * 48 + 48, :] = jnp.concatenate(
            [folded, jnp.zeros((6, COLS), F32)], axis=0
        )
    half_copy = pltpu.make_async_remote_copy(
        half_own, half_near, half_sems.at[0], half_sems.at[1], device_id=behind, device_id_type=MESH
    )
    half_copy.start()
    start_of = [0, 48, 12, 60, 24, 72, 36]
    for a in range(N):
        for b in range(N):
            d = (b - a) % N
            source = start_of[d] + a % (6 if d == 6 else N) if d < HALF else start_of[N - d] + b
            stiff_out[a * N + b] = half_own[source : source + 1, :]
    half_copy.wait()

    both = half_own[...] + moved(half_near[...])
    k = [both[s : s + (6 if d == 6 else N)] for d, s in enumerate(start_of)]
    k[0] = k[0] + 2.0

    resid = r_v[:, 0, :]
    precond = apply_half(k, resid)
    image = apply_full(own_c, precond)
    again = apply_half(k, image)
    image_again = apply_full(own_c, again)

    def inner(a, b):
        return jnp.sum(a * b, axis=0, keepdims=True)

    totals = jnp.concatenate(
        [inner(resid, precond), inner(precond, image), inner(image, again),
         inner(again, image_again)], axis=0,
    )
    totals = jnp.sum(totals, axis=1, keepdims=True)
    lane = lax.broadcasted_iota(I32, (1, COLS), 1)
    line = jnp.broadcast_to(unit, (1, COLS))
    for i in range(4):
        line = jnp.where(lane == i, totals[i : i + 1], line)
    mine[...] = line

    def spread(source, slots, here, steps, sems):
        count = len(steps) + 1
        slots[here] = source[...]
        for step in steps:
            pltpu.make_async_remote_copy(
                source, slots.at[here], sems.at[0], sems.at[1],
                device_id=at(**step), device_id_type=MESH,
            ).start()
        rest = slots.at[pl.ds(0, count - 1)]
        pltpu.make_async_copy(rest, rest, sems.at[1]).wait()
        return combine(slots[:, 0, :])

    def sent(slots, steps, sems):
        rest = slots.at[pl.ds(0, len(steps))]
        pltpu.make_async_copy(rest, rest, sems.at[0]).wait()

    row_steps = [dict(dz=dz, dc=dc) for dz, dc in ROW_STEPS]
    fan_steps = [dict(dy=dy, dx=dx) for dy, dx in FAN_STEPS]
    row_sum[...] = spread(mine, slots_a, zc, row_steps, sem_a)
    total = spread(row_sum, slots_b, y * GRP + grp, fan_steps, sem_b)
    rz, pq, quq, uw, top = (
        jnp.sum(jnp.where(lane == i, total, 0.0), axis=1, keepdims=True) for i in range(5)
    )
    alpha = rz / pq
    rz_next = alpha * alpha * quq - rz
    grown = 1.0 + rz_next / rz
    alpha_next = rz_next / (alpha * alpha * uw - grown * grown * pq)
    lam_out[:, 0, :] = (
        (alpha + alpha_next * grown) / top * precond
        - alpha_next * alpha / top * (unit / top) * again
    )
    sent(slots_a, row_steps, sem_a)
    sent(slots_b, fan_steps, sem_b)
    others = recv.at[pl.ds(0, SUB - 1)]
    pltpu.make_async_copy(others, others, sent_sem).wait()


def per_device(gradients, moduli, diag_terms, counts, targets, compliance, neighbours, rhs):
    vmem = lambda shape, dtype=F32: pltpu.VMEM(shape, dtype)
    dma = pltpu.SemaphoreType.DMA
    lam, stiff = pl.pallas_call(
        kernel,
        out_shape=(
            pltpu.VMEM((N, 1, COLS), F32),
            pltpu.VMEM((N * N, 1, COLS), F32),
        ),
        in_specs=[pl.BlockSpec(memory_space=pltpu.HBM)] * 8,
        out_specs=[pl.BlockSpec(memory_space=pltpu.VMEM)] * 2,
        scratch_shapes=[
            vmem((9, N, ELEMS), BF16),
            vmem((9, ELEMS), BF16),
            vmem((N, ELEMS), BF16),
            vmem((1, SUB), I32),
            vmem((1, ELEMS), I32),
            vmem((1, COLS), I32),
            vmem((N, 1, COLS)),
            vmem((N * N, COLS)),
            vmem((N * N, COLS)),
            vmem((LANES_OF, SLOT_ROWS, ELEMS), BF16),
            vmem((2 * COLS, ELEMS), BF16),
            vmem((SUB, ROWS_OF, COLS), I32),
            vmem((SUB, ROWS_OF, COLS), I32),
            vmem((96, COLS)),
            vmem((96, COLS)),
            vmem((1, COLS)),
            vmem((1, COLS)),
            vmem((ROW, 1, COLS)),
            vmem((COL * GRP, 1, COLS)),
            dma((8,)),
            pltpu.SemaphoreType.REGULAR((COL,)),
            dma((2,)),
            dma,
            dma((2,)),
            dma((2,)),
            dma((2,)),
            dma((2,)),
        ],
        compiler_params=pltpu.CompilerParams(
            collective_id=0, has_side_effects=True, vmem_limit_bytes=20 * 1024 * 1024
        ),
    )(
        *(
            pltpu.with_memory_space_constraint(operand, pltpu.HBM)
            for operand in (
                gradients[:, :, 0, :],
                moduli[:, 0, :],
                diag_terms[:, 0, :],
                counts[0],
                targets,
                compliance[:, 0, :],
                neighbours[0],
                rhs,
            )
        )
    )
    return pl.pallas_call(
        place,
        out_shape=(
            jax.ShapeDtypeStruct((N, 1, COLS), F32),
            jax.ShapeDtypeStruct((N * N, 1, COLS), F32),
        ),
        in_specs=[pl.BlockSpec(memory_space=pltpu.VMEM)] * 2,
        out_specs=[pl.BlockSpec(memory_space=pl.ANY)] * 2,
        scratch_shapes=[dma((2,))],
        compiler_params=pltpu.CompilerParams(vmem_limit_bytes=20 * 1024 * 1024),
    )(
        pltpu.with_memory_space_constraint(lam, pltpu.VMEM),
        pltpu.with_memory_space_constraint(stiff, pltpu.VMEM),
    )


def place(lam, stiff, lam_out, stiff_out, sems):
    copies = [
        pltpu.make_async_copy(stiff, stiff_out, sems.at[0]),
        pltpu.make_async_copy(lam, lam_out, sems.at[1]),
    ]
    for copy in copies:
        copy.start()
    for copy in copies:
        copy.wait()


def solution(mesh):
    in_specs = (
        P(None, None, "grp", "sub"),
        P(None, "grp", "sub"),
        P(None, "grp", "sub"),
        P("grp", "sub", None),
        P("grp", "sub"),
        P(None, "grp", "sub"),
        P("grp", "sub", None),
        P(None, "grp", "sub"),
    )
    out_specs = (P(None, "grp", "sub"), P(None, "grp", "sub"))
    return jax.shard_map(
        per_device, mesh=mesh, in_specs=in_specs, out_specs=out_specs, check_vma=False
    )
```
